512 devices in a mesh: group: 32 (over y, z_hi, core), mp: 16 (over z_lo, x).
Axes of the slice: x: 4, y: 4, z: 16 (z_hi: 4, z_lo: 4; z = z_hi * 4 + z_lo), core: 2. Of those that a mesh axis runs over, the one named last changes fastest.
Arguments:
- hidden: bfloat16 [8192, 8192], P('group', 'mp'), may hold values from -6 to 6
- targets: bfloat16 [8192, 4096], P('group', 'mp'), may hold values from -6 to 6
- counts: int32 [32, 4], P('group'), may hold values from 1 to 64, 160 in all within a row
- master: float32 [8192, 4096], P('group', 'mp'), may hold values from -3 to 3
Outputs:
- new_master: float32 [8192, 4096], P('group', 'mp')
- refreshed: bfloat16 [8192, 4096], P('group', 'mp')
The draws below stay inside these ranges and needn't reach their ends.
Inputs may be any that keep to these rules, and one draw needn't show every extreme that they name: Each serving group's counts sum to 160; in every group one sequence has exactly 64.
All inputs are finite; a program needn't handle non-finite values.
Results may differ from the reference program's by a relative error of at most 0.024.
Values may be sent and summed in bfloat16 or wider, within the bound.
A program may use at most 64 MiB of HBM per device.

```python
import math
import jax
import jax.numpy as jnp
import numpy as np
from jax import lax

D = 8192
F = 4096
SEQS = 4
SLOT = 64
CAP = 256
ROWS = 8192
N_GROUP = 32


def column_factor(key, low, high):
    place = jnp.arange(F, dtype=jnp.float32) / max(F - 1, 1)
    jitter = jax.random.uniform(jax.random.fold_in(key, 11), (F,), jnp.float32, 0.8, 1.25)
    return low * (high / low) ** place * jitter


def draw_master(key, part):
    factor = column_factor(key, 0.25, 1.0)
    key = jax.random.fold_in(key, 1)
    noise = jax.random.normal(key, (D, F), jnp.float32)
    return jnp.clip(0.5 * noise * factor[None, :], -3.0, 3.0).astype(jnp.float32)


def draw_targets(key, part):
    factor = column_factor(key, 0.25, 1.0)
    key = jax.random.fold_in(key, 2)
    noise = jax.random.normal(key, (ROWS, F), jnp.float32)
    return jnp.clip(noise * factor[None, :], -6.0, 6.0).astype(jnp.bfloat16)


def block_levels(own_key, extent, shards, low, high):
    def one(axis_at, blocks):
        steps = jax.random.uniform(jax.random.fold_in(jax.random.fold_in(own_key, 6), axis_at), (blocks,), jnp.float32, low / len(shards), high / len(shards))
        return jnp.repeat(jnp.exp(steps), extent[axis_at] // blocks).reshape((-1,) + (1,) * (len(extent) - axis_at - 1))

    level = one(*shards[0])
    for cut in shards[1:]:
        level = level * one(*cut)
    return level


def split_up(amount, total, most, slope):
    weights = [(1 << 20) // math.isqrt(grade ** slope) + 1 for grade in range(2, amount + 1)]
    rest, given = total - most - (amount - 1), [1] * (amount - 1)
    while rest > 0:
        candidates = [i for i in range(amount - 1) if given[i] < most]
        mass, remaining = sum([weights[i] for i in candidates]), rest
        for i in candidates:
            addition = min(most - given[i], max(1, remaining * weights[i] // mass), rest)
            given[i] = given[i] + addition
            rest = rest - addition
    return np.array([most] + given)


def uneven(own_key, count, total, most, skew):
    if count == 2:
        one = jax.random.randint(own_key, (), max(1, total - most), min(most, total - 1) + 1)
        return jnp.stack([one, total - one])
    sizes = jnp.asarray(split_up(count, total, most, skew), jnp.int32)
    pairs = (count - 1) // 2
    source_of, sink = sizes[1:1 + 2 * pairs:2], sizes[2:2 + 2 * pairs:2]
    slack = jnp.minimum(source_of - 1, most - sink)
    moved = jax.random.randint(jax.random.fold_in(own_key, 1), (pairs,), 0, 1 << 20) % (slack + 1)
    sizes = sizes.at[1:1 + 2 * pairs:2].set(source_of - moved).at[2:2 + 2 * pairs:2].set(sink + moved)
    return sizes[jax.random.permutation(jax.random.fold_in(own_key, 2), count)]


def scatter_about(rng, extent, width, limit, split=(), kind=jnp.bfloat16):
    gain = block_levels(rng, extent, split, -0.22, 0.18) if split else 1.0
    values = jax.random.normal(rng, extent, jnp.float32) * width * gain
    return jnp.minimum(jnp.maximum(values, -limit), limit).astype(kind)


def setup_inputs(seed: int = 0) -> dict:
    keys = jax.random.split(jax.random.key(seed), 5)
    return {
        "hidden": scatter_about(keys[0], (ROWS, D), 1.0, 6.0, ((0, 32), (1, 16))),
        "targets": draw_targets(jax.random.fold_in(keys[4], 71), 0),
        "counts": jax.vmap(lambda own: uneven(own, SEQS, SEQS * 40, SLOT, 1))(jax.random.split(keys[2], N_GROUP)).reshape((N_GROUP, SEQS)).astype(jnp.int32),
        "master": draw_master(jax.random.fold_in(keys[4], 71), 0),
    }


def reference(hidden, targets, counts, master):
    groups = counts.shape[0]
    scale = D ** (-0.5)
    weights16 = master.astype(jnp.bfloat16)
    pred = jnp.dot(hidden, weights16, preferred_element_type=jnp.float32) * scale
    valid = (jnp.arange(SLOT, dtype=jnp.int32)[None, None, :] < counts[:, :, None]).reshape(groups * CAP)
    diff = jnp.clip(pred - targets.astype(jnp.float32), -1.0, 1.0)
    err = (diff * valid[:, None].astype(jnp.float32)).astype(jnp.bfloat16)
    rows_g = hidden.reshape(groups, CAP, D)
    err_g = err.reshape(groups, CAP, F)

    def add_group(total, pair):
        part = lax.dot_general(pair[0], pair[1], (((0,), (0,)), ((), ())), preferred_element_type=jnp.float32) * scale
        part = lax.optimization_barrier(part.astype(jnp.bfloat16))
        return (total + part.astype(jnp.float32), None)
    grad, _ = lax.scan(add_group, jnp.zeros((D, F), jnp.float32), (rows_g, err_g))
    rms = jnp.sqrt(jnp.sum(grad * grad) / (D * F) + 1e-12)
    new_master = master - 0.25 * grad / rms
    renewed16 = new_master.astype(jnp.bfloat16)
    refreshed = (jnp.dot(hidden, renewed16, preferred_element_type=jnp.float32) * scale).astype(jnp.bfloat16)
    return (new_master, refreshed)
```

```python
import jax
import jax.numpy as jnp
from jax import lax
from jax.experimental import pallas as pl
from jax.experimental.pallas import tpu as pltpu
from jax.sharding import PartitionSpec as P

BF = jnp.bfloat16
F32 = jnp.float32
CAP = 256
SLOT = 64
LIVE = 160
REST = CAP - LIVE
B = 256
HB = B // 2
N_COPIES = 160


def shifted(at, **by):
    size = {"y": 4, "zh": 4, "c": 2, "zl": 4, "x": 4}
    return {k: lax.rem(v + by[k] + size[k], size[k]) if k in by else v for k, v in at.items()}


def device(at):
    return ((at["y"] * 4 + at["zh"]) * 2 + at["c"], at["zl"] * 4 + at["x"])


class Copies:
    def __init__(self, send_sem, recv_sem):
        self.send_sem, self.recv_sem, self.used, self.open = send_sem, recv_sem, 0, []

    def new(self, src, dst, to):
        at = self.used
        self.used += 1
        copy = pltpu.make_async_remote_copy(
            src_ref=src,
            dst_ref=dst,
            send_sem=self.send_sem.at[at],
            recv_sem=self.recv_sem.at[at],
            device_id=device(to),
            device_id_type=pl.DeviceIdType.MESH,
        )
        copy.start()
        self.open.append(copy)
        return copy

    def finish(self):
        for copy in self.open:
            copy.wait_send()


class Gather:
    def __init__(self, copies, at, axis, block, halves):
        self.copies, self.axis, self.block, self.halves = copies, axis, block, halves
        self.me = at[axis]
        self.right, self.left = shifted(at, **{axis: 1}), shifted(at, **{axis: -1})

    def start(self):
        mine = self.block(self.me)
        self.to_right = self.copies.new(mine, mine, self.right)
        self.to_left = self.copies.new(mine, mine, self.left)

    def hand_on(self):
        self.to_right.wait_recv()
        half = self.halves(self.block(lax.rem(self.me + 3, 4)))[0]
        self.on_right = self.copies.new(half, half, self.right)
        self.to_left.wait_recv()
        half = self.halves(self.block(lax.rem(self.me + 1, 4)))[1]
        self.on_left = self.copies.new(half, half, self.left)

    def end(self):
        self.on_right.wait_recv()
        self.on_left.wait_recv()


def row_halves(ref):
    return ref.at[pl.ds(0, HB)], ref.at[pl.ds(HB, HB)]


def core_halves(ref):
    return ref.at[0], ref.at[1]


def dot(a, b, contract=((1,), (0,))):
    return lax.dot_general(a, b, (contract, ((), ())), preferred_element_type=F32)


def place_of(row, counts):
    place = jnp.zeros_like(row)
    before = jnp.int32(0)
    for s in range(CAP // SLOT):
        count, inside = counts[s], row - s * SLOT
        valid = inside < count
        to = jnp.where(valid, before + inside, LIVE + s * SLOT - before + inside - count)
        place = jnp.where((row >= s * SLOT) & (row < (s + 1) * SLOT), to, place)
        before = before + count
    return place


def kernel(
    counts_ref, hidden_ref, targets_ref, master_ref, new_ref, out_ref,
    live, rest, cross_live, cross_rest, goal, goal_own, weights, half_pred, other_pred, err,
    part, y_first, y_sum, y_in, z_part, z_first, z_sum, z_in, grad, grad16,
    acc, rest_pred, to_other, from_other, square, squares,
    send_sem, recv_sem,
):
    group, mp = lax.axis_index("group"), lax.axis_index("mp")
    at = {
        "y": group // 8,
        "zh": lax.rem(group // 2, 4),
        "c": lax.rem(group, 2),
        "zl": mp // 4,
        "x": lax.rem(mp, 4),
    }
    y, zh, c, zl, x = at["y"], at["zh"], at["c"], at["zl"], at["x"]
    sibling = shifted(at, c=1)
    copies = Copies(send_sem, recv_sem)
    scale = (32 * B) ** (-0.5)

    barrier = pltpu.get_barrier_semaphore()
    near = [{"c": dc, "x": dx} for dc in range(2) for dx in range(4)][1:]
    stages = [near] + [[{axis: d} for d in (1, 2, 3)] for axis in ("y", "zl", "zh")]
    peers = [by for stage in stages for by in stage]
    for by in peers:
        pl.semaphore_signal(barrier, inc=1, device_id=device(shifted(at, **by)), device_id_type=pl.DeviceIdType.MESH)

    counts = [counts_ref[0, s] for s in range(CAP // SLOT)]
    source = lax.broadcasted_iota(jnp.int32, (CAP, CAP), 1)
    target = lax.broadcasted_iota(jnp.int32, (CAP, CAP), 0)
    to_front = jnp.where(place_of(source, counts) == target, 1.0, 0.0).astype(BF)
    low = dot(to_front, hidden_ref[:, :B]).astype(BF)
    high = dot(to_front, hidden_ref[:, B:]).astype(BF)
    mine, other = jnp.where(c == 0, low, high), jnp.where(c == 0, high, low)
    live[zl, x, c] = mine[:LIVE]
    rest[zl, x, c] = mine[LIVE:]
    cross_live[...] = other[:LIVE]
    cross_rest[...] = other[LIVE:]
    goal_own[...] = dot(to_front, targets_ref[...]).astype(BF)[:LIVE]
    weights[y, zh] = master_ref[...].astype(BF)
    pl.semaphore_wait(barrier, len(peers))

    swap_live = copies.new(cross_live, live.at[zl, x, c], sibling)
    swap_goal = copies.new(goal_own, goal.at[c], sibling)
    swap_rest = copies.new(cross_rest, rest.at[zl, x, c], sibling)

    def gather_rows(buffer):
        over_z = Gather(copies, at, "zh", lambda i: buffer.at[y, i], row_halves)
        over_y = [
            Gather(copies, at, "y", lambda i, k=k: buffer.at[i, lax.rem(zh + k, 4)], row_halves)
            for k in range(4)
        ]
        return over_z, over_y

    def gather_features(buffer):
        over_x = [
            Gather(copies, at, "x", lambda i, k=k: buffer.at[lax.rem(zl + k, 4), i], core_halves)
            for k in range(4)
        ]

        def line():
            mine = buffer.at[zl, x]
            return [copies.new(mine, mine, shifted(at, zl=d)) for d in (3, 2, 1)]

        return line, over_x

    wz, wy = gather_rows(weights)
    wz.start()
    wy[0].start()
    swap_live.wait_recv()
    line, hx = gather_features(live)
    hz = line()
    hx[0].start()
    wy[0].hand_on()
    hx[0].hand_on()
    hz[0].wait_recv()
    hx[1].start()
    hz[2].wait_recv()
    hx[3].start()
    wz.hand_on()
    wy[1].start()
    wy[3].start()
    hz[1].wait_recv()
    hx[2].start()
    hx[1].hand_on()
    hx[3].hand_on()
    wz.end()
    wy[2].start()
    wy[1].hand_on()
    wy[3].hand_on()
    hx[2].hand_on()
    wy[2].hand_on()
    for k in (0, 1, 3, 2):
        hx[k].end()
        wy[k].end()

    half_pred[...] = jnp.zeros_like(half_pred)

    @pl.loop(0, 16)
    def _(b):
        half_pred[...] += dot(live[b // 4, lax.rem(b, 4)].reshape(2 * LIVE, B), weights[b // 4, lax.rem(b, 4)])

    swap_pred = copies.new(half_pred, other_pred, sibling)
    swap_goal.wait_recv()
    goal[c] = goal_own[...]
    swap_pred.wait_recv()
    half_pred_total = half_pred[...] + other_pred[...]
    other_pred[...] = half_pred_total
    diff = jnp.clip(half_pred_total * scale - goal[...].reshape(2 * LIVE, B).astype(F32), -1.0, 1.0)
    err[...] = diff.astype(BF)

    swap_rest.wait_recv()
    rest_line, rx = gather_features(rest)

    def add(*terms):
        total = terms[0].astype(F32)
        for term in terms[1:]:
            total = total + term.astype(F32)
        return total

    def make_parts(k):
        zt = lax.rem(zh + k, 4)

        @pl.loop(0, 4)
        def _(yt):
            h = live[yt, zt].reshape(2 * LIVE, B)
            part[yt, zt] = (dot(h, err[...], ((0,), (0,))) * scale).astype(BF)

    up, down = shifted(at, y=1), shifted(at, y=-1)
    after, before = shifted(at, zh=1), shifted(at, zh=-1)
    yp, ym, yo = lax.rem(y + 1, 4), lax.rem(y + 3, 4), lax.rem(y + 2, 4)
    first, direct, second = {}, {}, {}

    def y_begin(k):
        zt = lax.rem(zh + k, 4)
        h0, h1 = row_halves(part.at[yo, zt])
        first[k] = (copies.new(h0, y_first.at[k, 0], up), copies.new(h1, y_first.at[k, 1], down))
        direct[k] = (
            copies.new(row_halves(part.at[yp, zt])[1], y_in.at[k, 0, 1], up),
            copies.new(row_halves(part.at[ym, zt])[0], y_in.at[k, 1, 0], down),
        )

    def y_middle(k):
        zt = lax.rem(zh + k, 4)
        first[k][0].wait_recv()
        y_sum[k, 0] = add(part[yp, zt, :HB], y_first[k, 0]).astype(BF)
        one = copies.new(y_sum.at[k, 0], y_in.at[k, 0, 0], up)
        first[k][1].wait_recv()
        y_sum[k, 1] = add(part[ym, zt, HB:], y_first[k, 1]).astype(BF)
        second[k] = (one, copies.new(y_sum.at[k, 1], y_in.at[k, 1, 1], down))

    def y_end(k):
        zt = lax.rem(zh + k, 4)
        for copy in direct[k] + second[k]:
            copy.wait_recv()
        total = add(part[y, zt], y_in[k, 0].reshape(B, B), y_in[k, 1].reshape(B, B))
        if k == 0:
            grad[...] = total
        else:
            z_part[k] = total.astype(BF)

    make_parts(2)
    y_begin(2)
    make_parts(1)
    y_begin(1)
    make_parts(3)
    y_begin(3)
    make_parts(0)
    y_middle(2)
    y_begin(0)
    y_end(2)
    h0, h1 = row_halves(z_part.at[2])
    z_first_copies = (copies.new(h0, z_first.at[0], after), copies.new(h1, z_first.at[1], before))
    rz = rest_line()
    rx[0].start()
    y_middle(1)
    y_middle(3)
    y_end(1)
    z_direct = [copies.new(row_halves(z_part.at[1])[1], z_in.at[0, 1], after)]
    y_end(3)
    z_direct.append(copies.new(row_halves(z_part.at[3])[0], z_in.at[1, 0], before))
    y_middle(0)
    z_first_copies[0].wait_recv()
    z_sum[0] = add(z_part[1, :HB], z_first[0]).astype(BF)
    z_direct.append(copies.new(z_sum.at[0], z_in.at[0, 0], after))
    z_first_copies[1].wait_recv()
    z_sum[1] = add(z_part[3, HB:], z_first[1]).astype(BF)
    z_direct.append(copies.new(z_sum.at[1], z_in.at[1, 1], before))
    y_end(0)
    rx[0].hand_on()
    rz[0].wait_recv()
    rx[1].start()
    rz[2].wait_recv()
    rx[3].start()
    rz[1].wait_recv()
    rx[2].start()
    rx[1].hand_on()
    rx[3].hand_on()
    for copy in z_direct:
        copy.wait_recv()
    grad[...] = add(grad[...], z_in[0].reshape(B, B), z_in[1].reshape(B, B))
    grad16[y, zh] = grad[...].astype(BF)

    gz, gy = gather_rows(grad16)
    gz.start()
    gy[0].start()

    total = jnp.sum(grad[...] * grad[...])
    square_copies = []

    def square_begin(s, total):
        square[s] = jnp.full((8, 128), total, F32)
        square_copies.append(
            [copies.new(square.at[s], squares.at[s, j], shifted(at, **by)) for j, by in enumerate(stages[s])]
        )

    def square_end(s):
        total = square[s]
        for j, copy in enumerate(square_copies[s]):
            copy.wait_recv()
            total = total + squares[s, j]
        return total[0, 0]

    square_begin(0, total)
    rx[2].hand_on()
    total = square_end(0)
    square_begin(1, total)
    gy[0].hand_on()
    total = square_end(1)
    square_begin(2, total)
    for k in range(4):
        rx[k].end()
    rest_pred[...] = jnp.zeros_like(rest_pred)
    acc[...] = jnp.zeros_like(acc)

    @pl.loop(0, 16)
    def _(b):
        rest_pred[...] += dot(rest[b // 4, lax.rem(b, 4)].reshape(2 * REST, B), weights[b // 4, lax.rem(b, 4)])

    def use(k):
        zt = lax.rem(zh + k, 4)

        @pl.loop(0, 4)
        def _(yt):
            g = grad16[yt, zt]
            acc[: 2 * LIVE] += dot(live[yt, zt].reshape(2 * LIVE, B), g)
            acc[2 * LIVE :] += dot(rest[yt, zt].reshape(2 * REST, B), g)

    total = square_end(2)
    square_begin(3, total)
    gz.hand_on()
    gy[1].start()
    gy[3].start()
    gy[0].end()
    use(0)
    gz.end()
    gy[2].start()
    gy[1].hand_on()
    gy[3].hand_on()
    total = square_end(3)
    rms = jnp.sqrt(jnp.full((8, 128), total, F32) / (32 * B * 16 * B) + 1e-12)
    step = (0.25 / rms)[0, 0]
    new_ref[...] = master_ref[...] - step * grad[...]
    gy[2].hand_on()
    for k in (1, 3, 2):
        gy[k].end()
        use(k)

    o = 1 - c
    live_at, rest_at = pl.multiple_of(c * LIVE, 8), pl.multiple_of(2 * LIVE + c * REST, 8)
    live_of, rest_of = pl.multiple_of(o * LIVE, 8), pl.multiple_of(2 * LIVE + o * REST, 8)
    to_other[:LIVE] = step * acc[pl.ds(live_of, LIVE)]
    to_other[LIVE:] = step * acc[pl.ds(rest_of, REST)] - rest_pred[pl.ds(pl.multiple_of(o * REST, 8), REST)]
    swap_out = copies.new(to_other, from_other, sibling)
    own_live = other_pred[pl.ds(live_at, LIVE)] - step * acc[pl.ds(live_at, LIVE)]
    own_rest = rest_pred[pl.ds(pl.multiple_of(c * REST, 8), REST)] - step * acc[pl.ds(rest_at, REST)]
    swap_out.wait_recv()
    own = jnp.concatenate([own_live - from_other[:LIVE], own_rest - from_other[LIVE:]], axis=0)
    out_ref[...] = dot(to_front, (own * scale).astype(BF), ((0,), (0,))).astype(BF)
    copies.finish()


def shards(hidden, targets, counts, master):
    vmem, bf, f32 = pltpu.VMEM, BF, F32
    return pl.pallas_call(
        kernel,
        out_shape=(jax.ShapeDtypeStruct((B, B), F32), jax.ShapeDtypeStruct((CAP, B), BF)),
        in_specs=[pl.BlockSpec(memory_space=pltpu.SMEM)] + [pl.BlockSpec(memory_space=vmem)] * 3,
        out_specs=[pl.BlockSpec(memory_space=vmem)] * 2,
        scratch_shapes=[
            vmem((4, 4, 2, LIVE, B), bf),
            vmem((4, 4, 2, REST, B), bf),
            vmem((LIVE, B), bf),
            vmem((REST, B), bf),
            vmem((2, LIVE, B), bf),
            vmem((LIVE, B), bf),
            vmem((4, 4, B, B), bf),
            vmem((2 * LIVE, B), f32),
            vmem((2 * LIVE, B), f32),
            vmem((2 * LIVE, B), bf),
            vmem((4, 4, B, B), bf),
            vmem((4, 2, HB, B), bf),
            vmem((4, 2, HB, B), bf),
            vmem((4, 2, 2, HB, B), bf),
            vmem((4, B, B), bf),
            vmem((2, HB, B), bf),
            vmem((2, HB, B), bf),
            vmem((2, 2, HB, B), bf),
            vmem((B, B), f32),
            vmem((4, 4, B, B), bf),
            vmem((2 * CAP, B), f32),
            vmem((2 * REST, B), f32),
            vmem((CAP, B), f32),
            vmem((CAP, B), f32),
            vmem((4, 8, 128), f32),
            vmem((4, 7, 8, 128), f32),
            pltpu.SemaphoreType.DMA((N_COPIES,)),
            pltpu.SemaphoreType.DMA((N_COPIES,)),
        ],
        compiler_params=pltpu.CompilerParams(
            collective_id=0, has_side_effects=True, vmem_limit_bytes=40 * 1024 * 1024
        ),
        name="recalibrate",
    )(counts, hidden, targets, master)


def solution(mesh):
    return jax.shard_map(
        shards,
        mesh=mesh,
        in_specs=(P("group", "mp"), P("group", "mp"), P("group", None), P("group", "mp")),
        out_specs=(P("group", "mp"), P("group", "mp")),
        check_vma=False,
    )
```

```python
import jax
import jax.numpy as jnp
from jax import lax
from jax.experimental import pallas as pl
from jax.experimental.pallas import tpu as pltpu
from jax.sharding import PartitionSpec as P

BF = jnp.bfloat16
F32 = jnp.float32
CAP = 256
SLOT = 64
LIVE = 160
REST = CAP - LIVE
B = 256
HB = B // 2
N = B // 2
N_COPIES = 256
MESH = pl.DeviceIdType.MESH


def shifted(at, **by):
    size = {"y": 4, "zh": 4, "c": 2, "zl": 4, "x": 4}
    return {k: lax.rem(v + by[k] + size[k], size[k]) if k in by else v for k, v in at.items()}


def device(at):
    return ((at["y"] * 4 + at["zh"]) * 2 + at["c"], at["zl"] * 4 + at["x"])


class Copies:
    def __init__(self, send_sem, recv_sem):
        self.send_sem, self.recv_sem, self.used, self.open, self.conditional = send_sem, recv_sem, 0, [], []

    def make(self, src, dst, to, recv_sem=None):
        at = self.used
        self.used += 1
        copy = pltpu.make_async_remote_copy(
            src_ref=src,
            dst_ref=dst,
            send_sem=self.send_sem.at[at],
            recv_sem=self.recv_sem.at[at] if recv_sem is None else recv_sem,
            device_id=device(to),
            device_id_type=MESH,
        )
        return copy

    def new(self, src, dst, to):
        copy = self.make(src, dst, to)
        copy.start()
        self.open.append(copy)
        return copy

    def new_if(self, condition, src, dst, to, recv_sem):
        copy = self.make(src, dst, to, recv_sem)
        pl.when(condition)(lambda: copy.start())
        self.conditional.append((condition, copy))

    def finish(self):
        for copy in self.open:
            copy.wait_send()
        for condition, copy in self.conditional:
            pl.when(condition)(lambda copy=copy: copy.wait_send())


class Gather:
    def __init__(self, copies, at, axis, block, halves, split=False):
        self.copies, self.block, self.halves, self.split = copies, block, halves, split
        self.me = at[axis]
        self.right, self.left = shifted(at, **{axis: 1}), shifted(at, **{axis: -1})
        self.of_left, self.of_right = lax.rem(self.me + 3, 4), lax.rem(self.me + 1, 4)

    def start(self):
        mine = self.block(self.me)
        if self.split:
            h0, h1 = self.halves(mine)
            self.to_right = self.copies.new(h0, h0, self.right)
            self.to_left = self.copies.new(h1, h1, self.left)
        else:
            self.to_right = self.copies.new(mine, mine, self.right)
            self.to_left = self.copies.new(mine, mine, self.left)

    def start_late(self):
        h0, h1 = self.halves(self.block(self.me))
        self.late = [self.copies.new(h1, h1, self.right), self.copies.new(h0, h0, self.left)]

    def hand_on(self):
        self.to_right.wait_recv()
        half = self.halves(self.block(self.of_left))[0]
        self.on_right = self.copies.new(half, half, self.right)
        self.to_left.wait_recv()
        half = self.halves(self.block(self.of_right))[1]
        self.on_left = self.copies.new(half, half, self.left)

    def near(self):
        for copy in self.late:
            copy.wait_recv()

    def end(self):
        self.on_right.wait_recv()
        self.on_left.wait_recv()


class Spread:
    def __init__(self, copies, at, axis, block):
        self.copies, self.mine = copies, block(at[axis])
        self.others = [shifted(at, **{axis: d}) for d in (1, 3, 2)]

    def start(self):
        self.sent = [self.copies.new(self.mine, self.mine, to) for to in self.others]

    def end(self):
        for copy in self.sent:
            copy.wait_recv()


class Line:
    def __init__(self, copies, at, block, sems):
        self.copies, self.at, self.block, self.sems = copies, at, block, sems
        zl = self.zl = at["zl"]
        self.middle = (zl == 1) | (zl == 2)
        low = zl == 1
        self.order = [
            jnp.where(zl == 0, 1, jnp.where(zl == 3, 3, jnp.where(low, 3, 1))),
            jnp.where(zl == 0, 2, jnp.where(zl == 3, 2, jnp.where(low, 1, 3))),
            jnp.where(zl == 0, 3, jnp.where(zl == 3, 1, 2)),
        ]
        self.step = [jnp.where(low, 1, -1), jnp.where(low, -1, 1), jnp.where(low, -1, 1)]
        self.lands = [2, 2, jnp.where(low, 3, 1)]

    def send(self, condition, zl, to, lands):
        ref = self.block(zl)
        self.copies.new_if(condition, ref, ref, {**self.at, "zl": to}, self.sems.at[lands])

    def start(self):
        zl = self.zl
        self.send(zl < 3, zl, lax.min(zl + 1, 3), 3)
        self.send(zl > 0, zl, lax.max(zl - 1, 0), 1)

    def slot(self, s):
        return lax.rem(self.zl + self.order[s], 4)

    def arrive(self, s):
        zl = self.slot(s)
        ref = self.block(zl)
        pltpu.make_async_copy(ref, ref, self.sems.at[self.order[s]]).wait()
        to = jnp.where(self.middle, self.zl + self.step[s], 1)
        self.send(self.middle, zl, to, self.lands[s])


def row_halves(ref):
    return ref.at[pl.ds(0, HB)], ref.at[pl.ds(HB, HB)]


def live_halves(ref):
    return ref.at[pl.ds(0, LIVE // 2)], ref.at[pl.ds(LIVE // 2, LIVE // 2)]


def dot(a, b, contract=((1,), (0,))):
    return lax.dot_general(a, b, (contract, ((), ())), preferred_element_type=F32)


def add(*terms):
    total = terms[0].astype(F32)
    for term in terms[1:]:
        total = total + term.astype(F32)
    return total


def place_of(row, counts):
    place = jnp.zeros_like(row)
    before = jnp.int32(0)
    for s in range(CAP // SLOT):
        count, inside = counts[s], row - s * SLOT
        valid = inside < count
        to = jnp.where(valid, before + inside, LIVE + s * SLOT - before + inside - count)
        place = jnp.where((row >= s * SLOT) & (row < (s + 1) * SLOT), to, place)
        before = before + count
    return place


def kernel(
    counts_ref, hidden_hbm, targets_hbm, master_hbm, new_ref, out_ref,
    hidden_ref, targets_ref, master_ref,
    live, rest, cross_live, cross_rest, goal, goal_own, weights, half_pred, other_pred, err,
    part, y_in, z_part, z_first, z_sum, z_in, grad, grad16,
    acc, rest_pred, to_other, from_other, square, squares,
    send_sem, recv_sem, line_sem, load_sem,
):
    group, mp = lax.axis_index("group"), lax.axis_index("mp")
    at = {
        "y": group // 8,
        "zh": lax.rem(group // 2, 4),
        "c": lax.rem(group, 2),
        "zl": mp // 4,
        "x": lax.rem(mp, 4),
    }
    y, zh, c, zl, x = at["y"], at["zh"], at["c"], at["zl"], at["x"]
    sibling = shifted(at, c=1)
    copies = Copies(send_sem, recv_sem)
    scale = (32 * B) ** (-0.5)

    barrier = pltpu.get_barrier_semaphore()
    near = [{"c": dc, "x": dx} for dc in range(2) for dx in range(4)][1:]
    stages = [near] + [[{axis: d} for d in (1, 2, 3)] for axis in ("y", "zl")]
    peers = [by for stage in stages for by in stage] + [{"zh": 1}, {"zh": -1}]
    for by in reversed(peers):
        pl.semaphore_signal(barrier, inc=1, device_id=device(shifted(at, **by)), device_id_type=MESH)
    loads = [
        pltpu.make_async_copy(src, dst, load_sem.at[i])
        for i, (src, dst) in enumerate(
            [(master_hbm, master_ref), (hidden_hbm, hidden_ref), (targets_hbm, targets_ref)]
        )
    ]
    for load in loads:
        load.start()
    loads[0].wait()
    for h in range(2):
        weights[h, y, zh] = master_ref[:, h * N : (h + 1) * N].astype(BF)

    def gather_rows(buffer, h):
        over_z = Gather(copies, at, "zh", lambda i: buffer.at[h, y, i], row_halves, split=True)
        over_y = [
            Spread(copies, at, "y", lambda i, k=k: buffer.at[h, i, lax.rem(zh + k, 4)]) for k in range(4)
        ]
        return over_z, over_y

    counts = [counts_ref[0, s] for s in range(CAP // SLOT)]
    place = place_of(lax.broadcasted_iota(jnp.int32, (8, CAP), 1), counts)[:1]
    target = lax.broadcasted_iota(jnp.int32, (CAP, CAP), 0)
    to_front = jnp.where(place == target, 1.0, 0.0).astype(BF)
    loads[1].wait()
    low = dot(to_front, hidden_ref[:, :B]).astype(BF)
    high = dot(to_front, hidden_ref[:, B:]).astype(BF)
    mine, other = jnp.where(c == 0, low, high), jnp.where(c == 0, high, low)
    cross_live[...] = other[:LIVE]
    cross_rest[...] = other[LIVE:]
    live[zl, x, c] = mine[:LIVE]
    rest[zl, x, c] = mine[LIVE:]
    (wz, wy), (vz, vy) = [gather_rows(weights, h) for h in range(2)]
    pl.semaphore_wait(barrier, len(peers))
    wz.start()
    wy[0].start()

    swap_live = copies.new(cross_live, live.at[zl, x, c], sibling)

    o = 1 - c
    a = Line(copies, at, lambda i: live.at[i, x, c], line_sem.at[0])
    b = Line(copies, at, lambda i: live.at[i, x, o], line_sem.at[1])
    places = [zl] + [a.slot(s) for s in range(3)]
    ax = [Gather(copies, at, "x", lambda i, p=p: live.at[p, i, c], live_halves) for p in places]
    bx = [Gather(copies, at, "x", lambda i, p=p: live.at[p, i, o], live_halves) for p in places]
    a.start()
    ax[0].start()
    loads[2].wait()
    goal_own[...] = dot(to_front, targets_ref[...]).astype(BF)[:LIVE]
    swap_goal = copies.new(goal_own, goal.at[c], sibling)
    swap_rest = copies.new(cross_rest, rest.at[zl, x, c], sibling)
    goal[c] = goal_own[...]
    swap_live.wait_recv()
    b.start()
    bx[0].start()
    wz.start_late()

    def predict(h):
        total = jnp.zeros((2 * LIVE, N), F32)
        for b in range(16):
            total = total + dot(live[b // 4, b % 4].reshape(2 * LIVE, B), weights[h, b // 4, b % 4])
        half_pred[h] = total
        return copies.new(half_pred.at[h], other_pred.at[h], sibling)

    def errors(h):
        total = half_pred[h] + other_pred[h]
        other_pred[h] = total
        wanted = goal[:, :, h * N : (h + 1) * N].reshape(2 * LIVE, N).astype(F32)
        err[h] = jnp.clip(total * scale - wanted, -1.0, 1.0).astype(BF)

    def predict_rest(h):
        total = jnp.zeros((2 * REST, N), F32)
        for b in range(16):
            total = total + dot(rest[b // 4, b % 4].reshape(2 * REST, B), weights[h, b // 4, b % 4])
        rest_pred[h] = total

    after, before = shifted(at, zh=1), shifted(at, zh=-1)

    class Reduce:
        def __init__(self, h):
            self.h, self.sent, self.z_direct = h, {}, []

        def parts(self, k):
            zt = lax.rem(zh + k, 4)
            e = err[self.h]
            for yt in range(4):
                rows = live[yt, zt].reshape(2 * LIVE, B)
                part[self.h, yt, zt] = (dot(rows, e, ((0,), (0,))) * scale).astype(BF)

        def begin(self, k):
            h, zt = self.h, lax.rem(zh + k, 4)
            self.sent[k] = [
                copies.new(part.at[h, lax.rem(y + d, 4), zt], y_in.at[h, k, d - 1], shifted(at, y=d))
                for d in (1, 3, 2)
            ]

        def end(self, k):
            h, zt = self.h, lax.rem(zh + k, 4)
            for copy in self.sent[k]:
                copy.wait_recv()
            total = add(part[h, y, zt], y_in[h, k, 0], y_in[h, k, 1], y_in[h, k, 2])
            if k == 0:
                grad[h] = total
                return
            z_part[h, k] = total.astype(BF)
            h0, h1 = row_halves(z_part.at[h, k])
            if k == 2:
                self.z_first = (
                    copies.new(h0, z_first.at[h, 0], after),
                    copies.new(h1, z_first.at[h, 1], before),
                )
            elif k == 1:
                self.z_direct.append(copies.new(h1, z_in.at[h, 0, 1], after))
            else:
                self.z_direct.append(copies.new(h0, z_in.at[h, 1, 0], before))

        def z_middle(self):
            h = self.h
            self.z_first[0].wait_recv()
            z_sum[h, 0] = add(z_part[h, 1, :HB], z_first[h, 0]).astype(BF)
            self.z_direct.append(copies.new(z_sum.at[h, 0], z_in.at[h, 0, 0], after))
            self.z_first[1].wait_recv()
            z_sum[h, 1] = add(z_part[h, 3, HB:], z_first[h, 1]).astype(BF)
            self.z_direct.append(copies.new(z_sum.at[h, 1], z_in.at[h, 1, 1], before))

        def z_end(self):
            h = self.h
            for copy in self.z_direct:
                copy.wait_recv()
            grad[h] = add(grad[h], z_in[h, 0].reshape(B, N), z_in[h, 1].reshape(B, N))
            grad16[h, y, zh] = grad[h].astype(BF)

    def use(h, k):
        zt = lax.rem(zh + k, 4)
        top = acc[h, : 2 * LIVE] if k else jnp.zeros((2 * LIVE, N), F32)
        low = acc[h, 2 * LIVE :] if k else jnp.zeros((2 * REST, N), F32)
        for yt in range(4):
            g = grad16[h, yt, zt]
            top = top + dot(live[yt, zt].reshape(2 * LIVE, B), g)
            low = low + dot(rest[yt, zt].reshape(2 * REST, B), g)
        acc[h, : 2 * LIVE] = top
        acc[h, 2 * LIVE :] = low

    a.arrive(0)
    ax[1].start()
    ax[0].hand_on()
    b.arrive(0)
    bx[1].start()
    bx[0].hand_on()
    wz.hand_on()
    vz.start()
    vy[0].start()
    a.arrive(1)
    ax[2].start()
    ax[1].hand_on()
    b.arrive(1)
    bx[2].start()
    bx[1].hand_on()
    wz.near()
    wy[1].start()
    wy[3].start()
    vz.start_late()
    a.arrive(2)
    ax[3].start()
    ax[2].hand_on()
    b.arrive(2)
    bx[3].start()
    bx[2].hand_on()
    wz.end()
    wy[2].start()
    vz.hand_on()
    ax[3].hand_on()
    bx[3].hand_on()
    for k in range(4):
        ax[k].end()
        bx[k].end()
        wy[k].end()

    swap_pred = predict(0)
    vz.near()
    vy[1].start()
    vy[3].start()
    swap_rest.wait_recv()
    swap_goal.wait_recv()
    rest_line = Line(copies, at, lambda i: rest.at[i, x], line_sem.at[2])
    rx = [Spread(copies, at, "x", lambda i, p=p: rest.at[p, i]) for p in places]
    rest_line.start()
    rx[0].start()
    swap_pred.wait_recv()
    errors(0)
    r0, r1 = Reduce(0), Reduce(1)
    r0.parts(2)
    r0.begin(2)
    r0.parts(1)
    r0.parts(3)
    r0.parts(0)
    vz.end()
    vy[2].start()
    r0.begin(1)
    r0.begin(3)
    r0.end(2)
    r0.begin(0)
    for k in range(4):
        vy[k].end()
    swap_pred = predict(1)
    rest_line.arrive(0)
    rx[1].start()
    r0.end(1)
    r0.end(3)
    swap_pred.wait_recv()
    errors(1)
    r1.parts(2)
    r1.begin(2)
    r0.z_middle()
    r1.parts(1)
    r1.parts(3)
    r1.parts(0)
    r1.begin(1)
    r1.begin(3)
    r0.end(0)
    r1.end(2)
    r1.begin(0)
    rest_line.arrive(1)
    rx[2].start()
    r0.z_end()
    (gz, gy), (fz, fy) = [gather_rows(grad16, h) for h in range(2)]
    gz.start()
    gz.start_late()
    gy[0].start()
    r1.end(1)
    r1.end(3)
    rest_line.arrive(2)
    rx[3].start()
    r1.z_middle()
    r1.end(0)
    gz.hand_on()
    gz.near()
    gy[1].start()
    gy[3].start()
    for k in range(4):
        rx[k].end()
    predict_rest(0)
    predict_rest(1)
    r1.z_end()
    fz.start()
    fz.start_late()
    fy[0].start()

    def square_begin(s, total):
        square[s] = jnp.full((8, 128), total, F32)
        return [copies.new(square.at[s], squares.at[s, j], shifted(at, **by)) for j, by in enumerate(stages[s])]

    def square_end(s, sent):
        total = square[s]
        for j, copy in enumerate(sent):
            copy.wait_recv()
            total = total + squares[s, j]
        return total[0, 0]

    total = jnp.sum(grad[0] * grad[0] + grad[1] * grad[1])
    sent = square_begin(0, total)
    gy[0].end()
    use(0, 0)
    gz.end()
    gy[2].start()
    sent = square_begin(1, square_end(0, sent))
    gy[1].end()
    use(0, 1)
    sent = square_begin(2, square_end(1, sent))
    gy[3].end()
    use(0, 3)
    fz.hand_on()
    total = square_end(2, sent)
    square[3] = jnp.full((8, 128), total, F32)
    ring = [copies.new(square.at[3], squares.at[3, 0], after), copies.new(square.at[3], squares.at[3, 1], before)]
    fz.near()
    fy[1].start()
    fy[3].start()
    gy[2].end()
    use(0, 2)
    fy[0].end()
    use(1, 0)
    ring[0].wait_recv()
    ring.append(copies.new(squares.at[3, 0], squares.at[3, 2], after))
    fz.end()
    fy[2].start()
    fy[1].end()
    use(1, 1)
    fy[3].end()
    use(1, 3)
    ring[1].wait_recv()
    ring[2].wait_recv()
    total = (square[3] + squares[3, 0]) + (squares[3, 1] + squares[3, 2])
    rms = jnp.sqrt(total / (32 * B * 16 * B) + 1e-12)
    step = (0.25 / rms)[0, 0]
    for h in range(2):
        new_ref[:, h * N : (h + 1) * N] = master_ref[:, h * N : (h + 1) * N] - step * grad[h]

    live_at, rest_at = pl.multiple_of(c * LIVE, 8), pl.multiple_of(c * REST, 8)
    live_of, rest_of = pl.multiple_of(o * LIVE, 8), pl.multiple_of(o * REST, 8)
    more = 2 * LIVE

    def give(h):
        to_other[h, :LIVE] = step * acc[h, pl.ds(live_of, LIVE)]
        to_other[h, LIVE:] = step * acc[h, pl.ds(more + rest_of, REST)] - rest_pred[h, pl.ds(rest_of, REST)]
        return copies.new(to_other.at[h], from_other.at[h], sibling)

    def take(h, swap):
        own_live = other_pred[h, pl.ds(live_at, LIVE)] - step * acc[h, pl.ds(live_at, LIVE)]
        own_rest = rest_pred[h, pl.ds(rest_at, REST)] - step * acc[h, pl.ds(more + rest_at, REST)]
        swap.wait_recv()
        own = jnp.concatenate([own_live - from_other[h, :LIVE], own_rest - from_other[h, LIVE:]], axis=0)
        out_ref[:, h * N : (h + 1) * N] = dot(to_front, (own * scale).astype(BF), ((0,), (0,))).astype(BF)

    take(0, give(0))
    fy[2].end()
    use(1, 2)
    take(1, give(1))
    copies.finish()


def shards(hidden, targets, counts, master):
    vmem, bf, f32 = pltpu.VMEM, BF, F32
    return pl.pallas_call(
        kernel,
        out_shape=(jax.ShapeDtypeStruct((B, B), F32), jax.ShapeDtypeStruct((CAP, B), BF)),
        in_specs=[pl.BlockSpec(memory_space=pltpu.SMEM)] + [pl.BlockSpec(memory_space=pl.ANY)] * 3,
        out_specs=[pl.BlockSpec(memory_space=vmem)] * 2,
        scratch_shapes=[
            vmem((CAP, 2 * B), bf),
            vmem((CAP, B), bf),
            vmem((B, B), f32),
            vmem((4, 4, 2, LIVE, B), bf),
            vmem((4, 4, 2, REST, B), bf),
            vmem((LIVE, B), bf),
            vmem((REST, B), bf),
            vmem((2, LIVE, B), bf),
            vmem((LIVE, B), bf),
            vmem((2, 4, 4, B, N), bf),
            vmem((2, 2 * LIVE, N), f32),
            vmem((2, 2 * LIVE, N), f32),
            vmem((2, 2 * LIVE, N), bf),
            vmem((2, 4, 4, B, N), bf),
            vmem((2, 4, 3, B, N), bf),
            vmem((2, 4, B, N), bf),
            vmem((2, 2, HB, N), bf),
            vmem((2, 2, HB, N), bf),
            vmem((2, 2, 2, HB, N), bf),
            vmem((2, B, N), f32),
            vmem((2, 4, 4, B, N), bf),
            vmem((2, 2 * CAP, N), f32),
            vmem((2, 2 * REST, N), f32),
            vmem((2, CAP, N), f32),
            vmem((2, CAP, N), f32),
            vmem((4, 8, 128), f32),
            vmem((4, 7, 8, 128), f32),
            pltpu.SemaphoreType.DMA((N_COPIES,)),
            pltpu.SemaphoreType.DMA((N_COPIES,)),
            pltpu.SemaphoreType.DMA((3, 4)),
            pltpu.SemaphoreType.DMA((3,)),
        ],
        compiler_params=pltpu.CompilerParams(
            collective_id=0, has_side_effects=True, vmem_limit_bytes=56 * 1024 * 1024
        ),
        name="recalibrate",
    )(counts, hidden, targets, master)


def solution(mesh):
    return jax.shard_map(
        shards,
        mesh=mesh,
        in_specs=(P("group", "mp"), P("group", "mp"), P("group", None), P("group", "mp")),
        out_specs=(P("group", "mp"), P("group", "mp")),
        check_vma=False,
    )
```

```python
import jax
import jax.numpy as jnp
from jax import lax
from jax.experimental import pallas as pl
from jax.experimental.pallas import tpu as pltpu
from jax.sharding import PartitionSpec as P

BF = jnp.bfloat16
F32 = jnp.float32
CAP = 256
SLOT = 64
LIVE = 160
REST = CAP - LIVE
B = 256
HB = B // 2
N = B // 2
N_COPIES = 256
MESH = pl.DeviceIdType.MESH


def shifted(at, **by):
    size = {"y": 4, "zh": 4, "c": 2, "zl": 4, "x": 4}
    return {k: lax.rem(v + by[k] + size[k], size[k]) if k in by else v for k, v in at.items()}


def device(at):
    return ((at["y"] * 4 + at["zh"]) * 2 + at["c"], at["zl"] * 4 + at["x"])


class Copies:
    def __init__(self, send_sem, recv_sem):
        self.send_sem, self.recv_sem, self.used, self.open, self.conditional = send_sem, recv_sem, 0, [], []

    def make(self, src, dst, to, recv_sem=None):
        at = self.used
        self.used += 1
        copy = pltpu.make_async_remote_copy(
            src_ref=src,
            dst_ref=dst,
            send_sem=self.send_sem.at[at],
            recv_sem=self.recv_sem.at[at] if recv_sem is None else recv_sem,
            device_id=device(to),
            device_id_type=MESH,
        )
        return copy

    def new(self, src, dst, to):
        copy = self.make(src, dst, to)
        copy.start()
        self.open.append(copy)
        return copy

    def new_if(self, condition, src, dst, to, recv_sem):
        copy = self.make(src, dst, to, recv_sem)
        pl.when(condition)(lambda: copy.start())
        self.conditional.append((condition, copy))

    def finish(self):
        for copy in self.open:
            copy.wait_send()
        for condition, copy in self.conditional:
            pl.when(condition)(lambda copy=copy: copy.wait_send())


class Gather:
    def __init__(self, copies, at, axis, block, halves, split=False):
        self.copies, self.block, self.halves, self.split = copies, block, halves, split
        self.me = at[axis]
        self.right, self.left = shifted(at, **{axis: 1}), shifted(at, **{axis: -1})
        self.of_left, self.of_right = lax.rem(self.me + 3, 4), lax.rem(self.me + 1, 4)

    def start(self):
        mine = self.block(self.me)
        if self.split:
            h0, h1 = self.halves(mine)
            self.to_right = self.copies.new(h0, h0, self.right)
            self.to_left = self.copies.new(h1, h1, self.left)
        else:
            self.to_right = self.copies.new(mine, mine, self.right)
            self.to_left = self.copies.new(mine, mine, self.left)

    def start_late(self):
        h0, h1 = self.halves(self.block(self.me))
        self.late = [self.copies.new(h1, h1, self.right), self.copies.new(h0, h0, self.left)]

    def hand_on(self):
        self.to_right.wait_recv()
        half = self.halves(self.block(self.of_left))[0]
        self.on_right = self.copies.new(half, half, self.right)
        self.to_left.wait_recv()
        half = self.halves(self.block(self.of_right))[1]
        self.on_left = self.copies.new(half, half, self.left)

    def near(self):
        for copy in self.late:
            copy.wait_recv()

    def end(self):
        self.on_right.wait_recv()
        self.on_left.wait_recv()


class Spread:
    def __init__(self, copies, at, axis, block):
        self.copies, self.mine = copies, block(at[axis])
        self.others = [shifted(at, **{axis: d}) for d in (1, 3, 2)]

    def start(self):
        self.sent = [self.copies.new(self.mine, self.mine, to) for to in self.others]

    def end(self):
        for copy in self.sent:
            copy.wait_recv()


class Line:
    def __init__(self, copies, at, block, sems):
        self.copies, self.at, self.block, self.sems = copies, at, block, sems
        zl = self.zl = at["zl"]
        self.middle = (zl == 1) | (zl == 2)
        low = zl == 1
        self.order = [
            jnp.where(zl == 0, 1, jnp.where(zl == 3, 3, jnp.where(low, 3, 1))),
            jnp.where(zl == 0, 2, jnp.where(zl == 3, 2, jnp.where(low, 1, 3))),
            jnp.where(zl == 0, 3, jnp.where(zl == 3, 1, 2)),
        ]
        self.step = [jnp.where(low, 1, -1), jnp.where(low, -1, 1), jnp.where(low, -1, 1)]
        self.lands = [2, 2, jnp.where(low, 3, 1)]

    def send(self, condition, zl, to, lands):
        ref = self.block(zl)
        self.copies.new_if(condition, ref, ref, {**self.at, "zl": to}, self.sems.at[lands])

    def start(self):
        zl = self.zl
        self.send(zl < 3, zl, lax.min(zl + 1, 3), 3)
        self.send(zl > 0, zl, lax.max(zl - 1, 0), 1)

    def slot(self, s):
        return lax.rem(self.zl + self.order[s], 4)

    def arrive(self, s):
        zl = self.slot(s)
        ref = self.block(zl)
        pltpu.make_async_copy(ref, ref, self.sems.at[self.order[s]]).wait()
        to = jnp.where(self.middle, self.zl + self.step[s], 1)
        self.send(self.middle, zl, to, self.lands[s])


def row_halves(ref):
    return ref.at[pl.ds(0, HB)], ref.at[pl.ds(HB, HB)]


def live_halves(ref):
    return ref.at[pl.ds(0, LIVE // 2)], ref.at[pl.ds(LIVE // 2, LIVE // 2)]


def dot(a, b, contract=((1,), (0,))):
    return lax.dot_general(a, b, (contract, ((), ())), preferred_element_type=F32)


def add(*terms):
    total = terms[0].astype(F32)
    for term in terms[1:]:
        total = total + term.astype(F32)
    return total


def place_of(row, counts):
    place = jnp.zeros_like(row)
    before = jnp.int32(0)
    for s in range(CAP // SLOT):
        count, inside = counts[s], row - s * SLOT
        valid = inside < count
        to = jnp.where(valid, before + inside, LIVE + s * SLOT - before + inside - count)
        place = jnp.where((row >= s * SLOT) & (row < (s + 1) * SLOT), to, place)
        before = before + count
    return place


def kernel(
    counts_ref, hidden_hbm, targets_hbm, master_hbm, new_ref, out_ref,
    hidden_ref, targets_ref, master_ref,
    live, rest, cross_live, cross_rest, goal, goal_own, weights, half_pred, other_pred, err,
    part, y_in, z_part, z_first, z_sum, z_in, grad, grad16,
    acc, rest_pred, to_other, from_other, square, squares,
    send_sem, recv_sem, line_sem, load_sem,
):
    group, mp = lax.axis_index("group"), lax.axis_index("mp")
    at = {
        "y": group // 8,
        "zh": lax.rem(group // 2, 4),
        "c": lax.rem(group, 2),
        "zl": mp // 4,
        "x": lax.rem(mp, 4),
    }
    y, zh, c, zl, x = at["y"], at["zh"], at["c"], at["zl"], at["x"]
    sibling = shifted(at, c=1)
    copies = Copies(send_sem, recv_sem)
    scale = (32 * B) ** (-0.5)

    barrier = pltpu.get_barrier_semaphore()
    near = [{"c": dc, "x": dx} for dc in range(2) for dx in range(4)][1:]
    stages = [near] + [[{axis: d} for d in (1, 2, 3)] for axis in ("y", "zl")]
    peers = [by for stage in stages for by in stage] + [{"zh": 1}, {"zh": -1}]
    for by in reversed(peers):
        pl.semaphore_signal(barrier, inc=1, device_id=device(shifted(at, **by)), device_id_type=MESH)
    loads = [
        pltpu.make_async_copy(src, dst, load_sem.at[i])
        for i, (src, dst) in enumerate(
            [(master_hbm, master_ref), (hidden_hbm, hidden_ref), (targets_hbm, targets_ref)]
        )
    ]
    for load in loads:
        load.start()
    loads[0].wait()
    for h in range(2):
        weights[h, y, zh] = master_ref[:, h * N : (h + 1) * N].astype(BF)

    def gather_rows(buffer, h):
        over_z = Gather(copies, at, "zh", lambda i: buffer.at[h, y, i], row_halves, split=True)
        over_y = [
            Spread(copies, at, "y", lambda i, k=k: buffer.at[h, i, lax.rem(zh + k, 4)]) for k in range(4)
        ]
        return over_z, over_y

    counts = [counts_ref[0, s] for s in range(CAP // SLOT)]
    place = place_of(lax.broadcasted_iota(jnp.int32, (8, CAP), 1), counts)[:1]
    target = lax.broadcasted_iota(jnp.int32, (CAP, CAP), 0)
    to_front = jnp.where(place == target, 1.0, 0.0).astype(BF)
    loads[1].wait()
    low = dot(to_front, hidden_ref[:, :B]).astype(BF)
    high = dot(to_front, hidden_ref[:, B:]).astype(BF)
    mine, other = jnp.where(c == 0, low, high), jnp.where(c == 0, high, low)
    cross_live[...] = other[:LIVE]
    cross_rest[...] = other[LIVE:]
    live[zl, x, c] = mine[:LIVE]
    rest[zl, x, c] = mine[LIVE:]
    (wz, wy), (vz, vy) = [gather_rows(weights, h) for h in range(2)]
    pl.semaphore_wait(barrier, len(peers))
    wz.start()
    wy[0].start()

    swap_live = copies.new(cross_live, live.at[zl, x, c], sibling)

    o = 1 - c
    a = Line(copies, at, lambda i: live.at[i, x, c], line_sem.at[0])
    b = Line(copies, at, lambda i: live.at[i, x, o], line_sem.at[1])
    places = [zl] + [a.slot(s) for s in range(3)]
    ax = [Gather(copies, at, "x", lambda i, p=p: live.at[p, i, c], live_halves) for p in places]
    bx = [Gather(copies, at, "x", lambda i, p=p: live.at[p, i, o], live_halves) for p in places]
    a.start()
    ax[0].start()
    loads[2].wait()
    goal_own[...] = dot(to_front, targets_ref[...]).astype(BF)[:LIVE]
    swap_goal = copies.new(goal_own, goal.at[c], sibling)
    swap_rest = copies.new(cross_rest, rest.at[zl, x, c], sibling)
    goal[c] = goal_own[...]
    swap_live.wait_recv()
    b.start()
    bx[0].start()
    wz.start_late()

    def predict(h):
        total = jnp.zeros((2 * LIVE, N), F32)
        for b in range(16):
            total = total + dot(live[b // 4, b % 4].reshape(2 * LIVE, B), weights[h, b // 4, b % 4])
        half_pred[h] = total
        return copies.new(half_pred.at[h], other_pred.at[h], sibling)

    def errors(h):
        total = half_pred[h] + other_pred[h]
        other_pred[h] = total
        wanted = goal[:, :, h * N : (h + 1) * N].reshape(2 * LIVE, N).astype(F32)
        err[h] = jnp.clip(total * scale - wanted, -1.0, 1.0).astype(BF)

    def predict_rest(h):
        total = jnp.zeros((2 * REST, N), F32)
        for b in range(16):
            total = total + dot(rest[b // 4, b % 4].reshape(2 * REST, B), weights[h, b // 4, b % 4])
        rest_pred[h] = total

    after, before = shifted(at, zh=1), shifted(at, zh=-1)

    class Reduce:
        def __init__(self, h):
            self.h, self.sent, self.z_direct = h, {}, []

        def parts(self, k):
            zt = lax.rem(zh + k, 4)
            e = err[self.h]
            for yt in range(4):
                rows = live[yt, zt].reshape(2 * LIVE, B)
                part[self.h, yt, zt] = (dot(rows, e, ((0,), (0,))) * scale).astype(BF)

        def begin(self, k):
            h, zt = self.h, lax.rem(zh + k, 4)
            self.sent[k] = [
                copies.new(part.at[h, lax.rem(y + d, 4), zt], y_in.at[h, k, d - 1], shifted(at, y=d))
                for d in (1, 3, 2)
            ]

        def end(self, k):
            h, zt = self.h, lax.rem(zh + k, 4)
            for copy in self.sent[k]:
                copy.wait_recv()
            total = add(part[h, y, zt], y_in[h, k, 0], y_in[h, k, 1], y_in[h, k, 2])
            if k == 0:
                grad[h] = total
                return
            z_part[h, k] = total.astype(BF)
            h0, h1 = row_halves(z_part.at[h, k])
            if k == 2:
                self.z_first = (
                    copies.new(h0, z_first.at[h, 0], after),
                    copies.new(h1, z_first.at[h, 1], before),
                )
            elif k == 1:
                self.z_direct.append(copies.new(h1, z_in.at[h, 0, 1], after))
            else:
                self.z_direct.append(copies.new(h0, z_in.at[h, 1, 0], before))

        def z_middle(self):
            h = self.h
            self.z_first[0].wait_recv()
            z_sum[h, 0] = add(z_part[h, 1, :HB], z_first[h, 0]).astype(BF)
            self.z_direct.append(copies.new(z_sum.at[h, 0], z_in.at[h, 0, 0], after))
            self.z_first[1].wait_recv()
            z_sum[h, 1] = add(z_part[h, 3, HB:], z_first[h, 1]).astype(BF)
            self.z_direct.append(copies.new(z_sum.at[h, 1], z_in.at[h, 1, 1], before))

        def z_end(self):
            h = self.h
            for copy in self.z_direct:
                copy.wait_recv()
            grad[h] = add(grad[h], z_in[h, 0].reshape(B, N), z_in[h, 1].reshape(B, N))
            grad16[h, y, zh] = grad[h].astype(BF)

    def use(h, k):
        zt = lax.rem(zh + k, 4)
        top = acc[h, : 2 * LIVE] if k else jnp.zeros((2 * LIVE, N), F32)
        low = acc[h, 2 * LIVE :] if k else jnp.zeros((2 * REST, N), F32)
        for yt in range(4):
            g = grad16[h, yt, zt]
            top = top + dot(live[yt, zt].reshape(2 * LIVE, B), g)
            low = low + dot(rest[yt, zt].reshape(2 * REST, B), g)
        acc[h, : 2 * LIVE] = top
        acc[h, 2 * LIVE :] = low

    a.arrive(0)
    ax[1].start()
    ax[0].hand_on()
    b.arrive(0)
    bx[1].start()
    bx[0].hand_on()
    wz.hand_on()
    vz.start()
    vy[0].start()
    a.arrive(1)
    ax[2].start()
    ax[1].hand_on()
    b.arrive(1)
    bx[2].start()
    bx[1].hand_on()
    wz.near()
    wy[1].start()
    wy[3].start()
    vz.start_late()
    a.arrive(2)
    ax[3].start()
    ax[2].hand_on()
    b.arrive(2)
    bx[3].start()
    bx[2].hand_on()
    wz.end()
    wy[2].start()
    vz.hand_on()
    ax[3].hand_on()
    bx[3].hand_on()
    vz.near()
    vy[1].start()
    vy[3].start()
    for k in range(4):
        ax[k].end()
        bx[k].end()
        wy[k].end()

    swap_pred = predict(0)
    swap_rest.wait_recv()
    swap_goal.wait_recv()
    vz.end()
    vy[2].start()
    rest_line = Line(copies, at, lambda i: rest.at[i, x], line_sem.at[2])
    rx = [Spread(copies, at, "x", lambda i, p=p: rest.at[p, i]) for p in places]
    rest_line.start()
    rx[0].start()
    swap_pred.wait_recv()
    errors(0)
    r0, r1 = Reduce(0), Reduce(1)
    r0.parts(2)
    r0.begin(2)
    r0.parts(1)
    r0.parts(3)
    r0.begin(1)
    r0.begin(3)
    r0.parts(0)
    for k in range(4):
        vy[k].end()
    swap_pred = predict(1)
    r0.end(2)
    r0.begin(0)
    swap_pred.wait_recv()
    errors(1)
    r1.parts(2)
    r1.begin(2)
    rest_line.arrive(0)
    rx[1].start()
    r0.end(1)
    r0.end(3)
    r1.parts(1)
    r1.parts(3)
    r1.parts(0)
    r0.z_middle()
    r1.begin(1)
    r1.begin(3)
    r0.end(0)
    r1.end(2)
    r1.begin(0)
    rest_line.arrive(1)
    rx[2].start()
    r0.z_end()
    (gz, gy), (fz, fy) = [gather_rows(grad16, h) for h in range(2)]
    gz.start()
    gz.start_late()
    gy[0].start()
    r1.end(1)
    r1.end(3)
    rest_line.arrive(2)
    rx[3].start()
    r1.z_middle()
    r1.end(0)
    gz.hand_on()
    gz.near()
    gy[1].start()
    gy[3].start()
    for k in range(4):
        rx[k].end()
    predict_rest(0)
    predict_rest(1)
    r1.z_end()
    fz.start()
    fy[0].start()

    def square_begin(s, total):
        square[s] = jnp.full((8, 128), total, F32)
        return [copies.new(square.at[s], squares.at[s, j], shifted(at, **by)) for j, by in enumerate(stages[s])]

    def square_end(s, sent):
        total = square[s]
        for j, copy in enumerate(sent):
            copy.wait_recv()
            total = total + squares[s, j]
        return total[0, 0]

    total = jnp.sum(grad[0] * grad[0] + grad[1] * grad[1])
    sent = square_begin(0, total)
    gy[0].end()
    use(0, 0)
    fz.start_late()
    gz.end()
    gy[2].start()
    sent = square_begin(1, square_end(0, sent))
    gy[1].end()
    use(0, 1)
    sent = square_begin(2, square_end(1, sent))
    gy[3].end()
    use(0, 3)
    fz.hand_on()
    total = square_end(2, sent)
    square[3] = jnp.full((8, 128), total, F32)
    ring = [copies.new(square.at[3], squares.at[3, 0], after), copies.new(square.at[3], squares.at[3, 1], before)]
    fz.near()
    fy[1].start()
    fy[3].start()
    gy[2].end()
    use(0, 2)
    fy[0].end()
    use(1, 0)
    ring[0].wait_recv()
    ring.append(copies.new(squares.at[3, 0], squares.at[3, 2], after))
    fz.end()
    fy[2].start()
    fy[1].end()
    use(1, 1)
    fy[3].end()
    use(1, 3)
    ring[1].wait_recv()
    ring[2].wait_recv()
    total = (square[3] + squares[3, 0]) + (squares[3, 1] + squares[3, 2])
    rms = jnp.sqrt(total / (32 * B * 16 * B) + 1e-12)
    step = (0.25 / rms)[0, 0]
    for h in range(2):
        new_ref[:, h * N : (h + 1) * N] = master_ref[:, h * N : (h + 1) * N] - step * grad[h]

    live_at, rest_at = pl.multiple_of(c * LIVE, 8), pl.multiple_of(c * REST, 8)
    live_of, rest_of = pl.multiple_of(o * LIVE, 8), pl.multiple_of(o * REST, 8)
    more = 2 * LIVE

    def give(h):
        to_other[h, :LIVE] = step * acc[h, pl.ds(live_of, LIVE)]
        to_other[h, LIVE:] = step * acc[h, pl.ds(more + rest_of, REST)] - rest_pred[h, pl.ds(rest_of, REST)]
        return copies.new(to_other.at[h], from_other.at[h], sibling)

    def take(h, swap):
        own_live = other_pred[h, pl.ds(live_at, LIVE)] - step * acc[h, pl.ds(live_at, LIVE)]
        own_rest = rest_pred[h, pl.ds(rest_at, REST)] - step * acc[h, pl.ds(more + rest_at, REST)]
        swap.wait_recv()
        own = jnp.concatenate([own_live - from_other[h, :LIVE], own_rest - from_other[h, LIVE:]], axis=0)
        out_ref[:, h * N : (h + 1) * N] = dot(to_front, (own * scale).astype(BF), ((0,), (0,))).astype(BF)

    take(0, give(0))
    fy[2].end()
    use(1, 2)
    take(1, give(1))
    copies.finish()


def shards(hidden, targets, counts, master):
    vmem, bf, f32 = pltpu.VMEM, BF, F32
    return pl.pallas_call(
        kernel,
        out_shape=(jax.ShapeDtypeStruct((B, B), F32), jax.ShapeDtypeStruct((CAP, B), BF)),
        in_specs=[pl.BlockSpec(memory_space=pltpu.SMEM)] + [pl.BlockSpec(memory_space=pl.ANY)] * 3,
        out_specs=[pl.BlockSpec(memory_space=vmem)] * 2,
        scratch_shapes=[
            vmem((CAP, 2 * B), bf),
            vmem((CAP, B), bf),
            vmem((B, B), f32),
            vmem((4, 4, 2, LIVE, B), bf),
            vmem((4, 4, 2, REST, B), bf),
            vmem((LIVE, B), bf),
            vmem((REST, B), bf),
            vmem((2, LIVE, B), bf),
            vmem((LIVE, B), bf),
            vmem((2, 4, 4, B, N), bf),
            vmem((2, 2 * LIVE, N), f32),
            vmem((2, 2 * LIVE, N), f32),
            vmem((2, 2 * LIVE, N), bf),
            vmem((2, 4, 4, B, N), bf),
            vmem((2, 4, 3, B, N), bf),
            vmem((2, 4, B, N), bf),
            vmem((2, 2, HB, N), bf),
            vmem((2, 2, HB, N), bf),
            vmem((2, 2, 2, HB, N), bf),
            vmem((2, B, N), f32),
            vmem((2, 4, 4, B, N), bf),
            vmem((2, 2 * CAP, N), f32),
            vmem((2, 2 * REST, N), f32),
            vmem((2, CAP, N), f32),
            vmem((2, CAP, N), f32),
            vmem((4, 8, 128), f32),
            vmem((4, 7, 8, 128), f32),
            pltpu.SemaphoreType.DMA((N_COPIES,)),
            pltpu.SemaphoreType.DMA((N_COPIES,)),
            pltpu.SemaphoreType.DMA((3, 4)),
            pltpu.SemaphoreType.DMA((3,)),
        ],
        compiler_params=pltpu.CompilerParams(
            collective_id=0, has_side_effects=True, vmem_limit_bytes=56 * 1024 * 1024
        ),
        name="recalibrate",
    )(counts, hidden, targets, master)


def solution(mesh):
    return jax.shard_map(
        shards,
        mesh=mesh,
        in_specs=(P("group", "mp"), P("group", "mp"), P("group", None), P("group", "mp")),
        out_specs=(P("group", "mp"), P("group", "mp")),
        check_vma=False,
    )
```
